32 devices in a mesh: states: 16 (over z, y, x), act: 2 (over core).
Axes of the slice: x: 2, y: 2, z: 4, core: 2. Of those that a mesh axis runs over, the one named last changes fastest.
Arguments:
- transitions: float32 [4, 256, 2, 128, 128], P('act', 'states'), may hold values from 7.8125e-05 to 0.01953125
- columns: int32 [4, 256, 2], P(None, 'states'), may hold values from 0 to 255, as said below
- targets: int32 [32768, 128], P('states'), may hold values 0 or 1
Outputs:
- values: float32 [32768, 128], P('states')
The draws below stay inside these ranges and needn't reach their ends.
Inputs may be any that keep to these rules, and one draw needn't show every extreme that they name: columns[a, b, t] = (b + d) mod 256 with |d| <= 8; both d = 8 and d = -8 occur in every draw.
All inputs are finite; a program needn't handle non-finite values. No bound on the sum of `targets` on one device may be relied on, other than what follows from the above.
Results may differ from the reference program's by a relative error of at most 0.0003.
Values sent between devices are 32-bit elements; how exact they have to be, the bound alone decides.
No kernel may reach another device: no remote copies, remote signals or barrier semaphores. Data moves between devices by JAX's collectives and lax.ppermute only.
A program may use at most 64 MiB of HBM per device.

```python
import math
import jax
import jax.numpy as jnp
from jax import lax

TILE = 128
K = 128
ACTIONS = 4
REACH = 8
SWEEPS = 12
RB_DEV = 16
BLOCKS = 256
NSTATES = 32768


def draw_columns(key, part):
    offsets = jax.random.randint(key, (ACTIONS, BLOCKS, 2), -REACH, REACH + 1)
    upper_rows = jax.random.randint(jax.random.fold_in(key, 11), (ACTIONS,), 0, BLOCKS)
    lower_rows = jax.random.randint(jax.random.fold_in(key, 12), (ACTIONS,), 0, BLOCKS)
    action_ids = jnp.arange(ACTIONS, dtype=jnp.int32)
    offsets = offsets.at[action_ids, upper_rows, 0].set(REACH)
    offsets = offsets.at[action_ids, lower_rows, 1].set(-REACH)
    row_ids = jnp.arange(BLOCKS, dtype=jnp.int32)[None, :, None]
    return ((row_ids + offsets) % BLOCKS).astype(jnp.int32)


def set_ends(result, stream_key, least, high):
    longest = result.shape.index(max(result.shape))
    spots = []
    for shift in (0, 1):
        where = [jax.random.randint(jax.random.fold_in(stream_key, axis), (), 0, length) for axis, length in enumerate(result.shape)]
        where[longest] = (where[longest] + shift) % result.shape[longest]
        spots.append(tuple(where))
    return result.at[spots[0]].set(least).at[spots[1]].set(high)


def steps_of(rng, dims, split, low, high):
    level = 1.0
    for dim, shards_of in split:
        heights = jax.random.uniform(jax.random.fold_in(jax.random.fold_in(rng, 6), dim), (shards_of,), jnp.float32, low / len(split), high / len(split))
        level = level * jnp.repeat(jnp.exp(heights), dims[dim] // shards_of).reshape((-1,) + (1,) * (len(dims) - 1 - dim))
    return level


def setup_inputs(seed: int = 0) -> dict:
    seeds = jax.random.split(jax.random.key(seed), 4)
    transitions = jnp.clip(jnp.exp(math.log(0.01953125) - 5.521461 * jax.random.uniform(seeds[0], (ACTIONS, BLOCKS, 2, TILE, TILE), jnp.float32) ** steps_of(seeds[0], (ACTIONS, BLOCKS, 2, TILE, TILE), ((0, 2), (1, 16)), -0.2, 0.2)), 7.812499825377017e-05, 0.01953125)
    columns = draw_columns(jax.random.fold_in(seeds[3], 71), 0)
    targets = set_ends((jax.random.randint(seeds[2], (NSTATES, K), 0, 8) < 1).astype(jnp.int32), jax.random.fold_in(seeds[2], 1), 0, 1)
    return {"transitions": transitions, "columns": columns, "targets": targets}


def reference(transitions, columns, targets):
    hits = targets == 1
    panel = targets.astype(jnp.float32)
    group_count = BLOCKS // RB_DEV
    for sweep_index in range(SWEEPS):
        blocks = panel.reshape(BLOCKS, TILE, K)

        def one_group(group_index):
            first_row = (group_index * RB_DEV).astype(jnp.int32)
            tiles = lax.dynamic_slice_in_dim(transitions, first_row, RB_DEV, 1)
            column_ids = lax.dynamic_slice_in_dim(columns, first_row, RB_DEV, 1)
            picked = blocks[column_ids]
            products = jnp.einsum("arbij,arbjk->arik", tiles, picked, precision=lax.Precision.HIGHEST)
            return jnp.max(products, axis=0)

        largest = lax.map(one_group, jnp.arange(group_count, dtype=jnp.int32))
        panel = jnp.where(hits, jnp.float32(1.0), largest.reshape(NSTATES, K))
    return panel
```

```python
import functools

import jax
import jax.numpy as jnp
from jax import lax
from jax.experimental import pallas as pl
from jax.experimental.pallas import tpu as pltpu
from jax.sharding import PartitionSpec as P

REACH = 8
SWEEPS = 12
CHUNKS = 2
AXES = ("states", "act")
VMEM = pltpu.VMEM
SMEM = pltpu.SMEM


def in_vmem(x):
    return pltpu.with_memory_space_constraint(x, VMEM)


def split(x):
    high = x.astype(jnp.bfloat16)
    return high, (x - high.astype(jnp.float32)).astype(jnp.bfloat16)


def turn_targets(own_ref, out_refs):
    blocks, width, lanes = out_refs[0].shape
    for b in range(blocks):
        turned = own_ref[b * lanes : (b + 1) * lanes, :].astype(jnp.float32).T
        for c, out_ref in enumerate(out_refs):
            out_ref[b] = turned[c * width : (c + 1) * width, :]


def start_kernel(own_ref, sib_ref, *out_refs):
    turn_targets(own_ref, out_refs[:CHUNKS])
    turn_targets(sib_ref, out_refs[CHUNKS:])


def tiles_kernel(tiles_ref, out_ref):
    actions = tiles_ref.shape[0]
    lanes = tiles_ref.shape[-1]
    for a in range(actions):
        for t in range(2):
            high, low = split(tiles_ref[a, 0, t].T)
            out_ref[0, a, t * lanes : (t + 1) * lanes, :lanes] = high
            out_ref[0, a, t * lanes : (t + 1) * lanes, lanes:] = low


def sweep_kernel(slot_ref, first_ref, second_ref, own_ref, sib_ref, ici_ref, target_ref, out_ref, parts_ref):
    blocks, width, lanes = own_ref.shape
    for n, ref in enumerate((own_ref, sib_ref, ici_ref)):
        for b in range(blocks):
            high, low = split(ref[b])
            parts_ref[n * blocks + b, :width] = high
            parts_ref[n * blocks + b, width:] = low
    for b in range(blocks):
        largest = None
        for n, tiles_ref in enumerate((first_ref, second_ref)):
            for a in range(tiles_ref.shape[1]):
                at = (n * tiles_ref.shape[1] + a) * blocks * 2 + b * 2
                left = jnp.concatenate([parts_ref[slot_ref[at]], parts_ref[slot_ref[at + 1]]], axis=1)
                both = jnp.dot(left, tiles_ref[b, a], preferred_element_type=jnp.float32)
                q = (both[:width, :lanes] + both[:width, lanes:]) + (both[width:, :lanes] + both[width:, lanes:])
                largest = q if largest is None else jnp.maximum(largest, q)
        out_ref[b] = jnp.where(target_ref[b] == 1.0, 1.0, largest)


def finish_kernel(core_ref, *refs):
    own_refs, sib_refs, out_ref = refs[:CHUNKS], refs[CHUNKS:-1], refs[-1]
    blocks, width, lanes = own_refs[0].shape
    core = core_ref[0]
    for part, group in ((core, own_refs), (1 - core, sib_refs)):
        for b in range(blocks):
            panel = jnp.concatenate([ref[b] for ref in group], axis=0)
            out_ref[pl.ds(pl.multiple_of(part * (blocks * lanes) + b * lanes, lanes), lanes), :] = panel.T


def per_device(transitions, columns, targets):
    acts_here, row_blocks, _, lanes, _ = transitions.shape
    sets = targets.shape[1]
    width = sets // CHUNKS
    blocks = row_blocks // 2
    rows = blocks * lanes
    states = lax.axis_size("states")
    total_blocks = row_blocks * states
    devices = 2 * states
    core = lax.axis_index("act")
    first_block = lax.axis_index("states") * row_blocks + core * blocks

    to_sib = [(i, i ^ 1) for i in range(devices)]
    to_ici = [(i, (i + 1) % devices if i % 2 else (i - 1) % devices) for i in range(devices)]

    chunk = jax.ShapeDtypeStruct((blocks, width, lanes), jnp.float32)
    whole = pl.BlockSpec(memory_space=VMEM)
    scalars = pl.BlockSpec(memory_space=SMEM)

    half = lambda which: pl.BlockSpec((rows, sets), lambda i, core_ref: (which(core_ref[0]), 0))
    core_arr = core.astype(jnp.int32).reshape(1)
    started = pl.pallas_call(
        lambda core_ref, own_ref, sib_ref, *outs: start_kernel(own_ref, sib_ref, *outs),
        out_shape=[chunk] * (2 * CHUNKS),
        grid_spec=pltpu.PrefetchScalarGridSpec(
            num_scalar_prefetch=1,
            grid=(1,),
            in_specs=[half(lambda c: c), half(lambda c: 1 - c)],
            out_specs=[pl.BlockSpec((blocks, width, lanes), lambda i, core_ref: (0, 0, 0))] * (2 * CHUNKS),
        ),
        name="start",
    )(core_arr, targets, targets)
    zero, sib = list(started[:CHUNKS]), list(started[CHUNKS:])
    ici = [lax.ppermute(v, AXES, to_ici) for v in zero]

    given = lax.dynamic_slice_in_dim(transitions, (1 - core) * blocks, blocks, 1)
    taken = lax.ppermute(given, AXES, to_sib)

    def right_sides(tiles, offset):
        return pl.pallas_call(
            lambda offset_ref, tiles_ref, out_ref: tiles_kernel(tiles_ref, out_ref),
            out_shape=jax.ShapeDtypeStruct((blocks, acts_here, 2 * lanes, 2 * lanes), jnp.bfloat16),
            grid_spec=pltpu.PrefetchScalarGridSpec(
                num_scalar_prefetch=1,
                grid=(blocks,),
                in_specs=[pl.BlockSpec((acts_here, 1, 2, lanes, lanes), lambda i, offset_ref: (0, offset_ref[0] + i, 0, 0, 0))],
                out_specs=pl.BlockSpec((1, acts_here, 2 * lanes, 2 * lanes), lambda i, offset_ref: (i, 0, 0, 0)),
            ),
            name="tiles",
        )(offset, tiles)

    first = right_sides(transitions, core_arr * blocks)
    second = right_sides(taken, jnp.zeros((1,), jnp.int32))

    mine = lax.dynamic_slice_in_dim(columns, core * blocks, blocks, 1)
    mine = jnp.concatenate(
        [lax.dynamic_slice_in_dim(mine, core * acts_here, acts_here, 0), lax.dynamic_slice_in_dim(mine, (1 - core) * acts_here, acts_here, 0)]
    )
    place = (mine - first_block + blocks) % total_blocks
    left = place + jnp.where(core == 0, 2 * blocks, blocks)
    right = place - 2 * blocks + jnp.where(core == 0, blocks, 2 * blocks)
    slots = jnp.where(place < blocks, left, jnp.where(place < 2 * blocks, place - blocks, right)).reshape(-1)

    def sweep(own, sib, ici, zero):
        return pl.pallas_call(
            sweep_kernel,
            out_shape=chunk,
            in_specs=[scalars] + [whole] * 6,
            out_specs=whole,
            scratch_shapes=[pltpu.VMEM((3 * blocks, 2 * width, lanes), jnp.bfloat16)],
            name="sweep",
            compiler_params=pltpu.CompilerParams(vmem_limit_bytes=24 << 20),
            cost_estimate=pl.CostEstimate(
                flops=2 * 2 * acts_here * blocks * (2 * width) * (2 * lanes) ** 2,
                bytes_accessed=4 * 5 * blocks * width * lanes + 8 * acts_here * blocks * (2 * lanes) ** 2,
                transcendentals=0,
            ),
        )(slots, first, second, own, sib, ici, zero)

    own = list(zero)
    for step in range(SWEEPS):
        for c in range(CHUNKS):
            own[c] = sweep(own[c], sib[c], ici[c], zero[c])
            if step < SWEEPS - 1:
                ici[c] = lax.ppermute(own[c], AXES, to_ici)
            sib[c] = lax.ppermute(own[c], AXES, to_sib)

    return pl.pallas_call(
        finish_kernel,
        out_shape=jax.ShapeDtypeStruct((2 * rows, sets), jnp.float32),
        in_specs=[scalars] + [whole] * (2 * CHUNKS),
        out_specs=whole,
        name="finish",
    )(core_arr, *own, *sib)


def solution(mesh):
    return jax.shard_map(
        per_device,
        mesh=mesh,
        in_specs=(P("act", "states", None, None, None), P(None, "states", None), P("states", None)),
        out_specs=P("states", None),
        check_vma=False,
    )
```

```python
import functools

import jax
import jax.numpy as jnp
from jax import lax
from jax.experimental import pallas as pl
from jax.experimental.pallas import tpu as pltpu
from jax.sharding import PartitionSpec as P

SWEEPS = 12
CHUNKS = 2
AXES = ("states", "act")
VMEM = pltpu.VMEM
SMEM = pltpu.SMEM
HBM = pltpu.HBM
WHOLE = pl.BlockSpec(memory_space=VMEM)
SCALARS = pl.BlockSpec(memory_space=SMEM)
ANYWHERE = pl.BlockSpec(memory_space=pl.ANY)


def split(x):
    high = x.astype(jnp.bfloat16)
    return high, (x - high.astype(jnp.float32)).astype(jnp.bfloat16)


def unit(rows, repeats=1):
    row = lax.broadcasted_iota(jnp.int32, (rows, rows), 0)
    col = lax.broadcasted_iota(jnp.int32, (rows, rows), 1)
    one = jnp.where(row == col, 1.0, 0.0).astype(jnp.bfloat16)
    return jnp.concatenate([one] * repeats, axis=1)


def times_turned(left, right):
    return lax.dot_general(left, right, (((1,), (1,)), ((), ())), preferred_element_type=jnp.float32)


def turn_targets(held_ref, out_refs):
    blocks, width, lanes = out_refs[0].shape
    one = unit(held_ref.shape[1])
    for b in range(blocks):
        hit = held_ref[b * lanes : (b + 1) * lanes, :].astype(jnp.float32).astype(jnp.bfloat16)
        turned = times_turned(one, hit)
        for c, out_ref in enumerate(out_refs):
            out_ref[b] = turned[c * width : (c + 1) * width, :]


def half_of(ref, part):
    rows = ref.shape[0] // 2
    return ref.at[pl.ds(pl.multiple_of(part * rows, rows), rows)]


def own_kernel(targets_ref, *refs):
    out_refs, (held_ref, sem) = refs[:CHUNKS], refs[CHUNKS:]
    copy = pltpu.make_async_copy(half_of(targets_ref, lax.axis_index("act")), held_ref, sem)
    copy.start()
    copy.wait()
    turn_targets(held_ref, out_refs)


def turn_tiles(tiles_ref, first, out_ref, start):
    blocks, _, side, _ = out_ref.shape
    lanes = side // 2
    one = unit(lanes)
    for b in range(blocks):
        for a in range(tiles_ref.shape[0]):
            for t in range(2):
                both = jnp.concatenate(split(tiles_ref[a, first + b, t]), axis=0)
                out_ref[b, start + a, t * lanes : (t + 1) * lanes] = times_turned(one, both).astype(jnp.bfloat16)


def rest_kernel(columns_ref, targets_ref, tiles_ref, taken_ref, slots_ref, right_ref, *refs):
    out_refs, (held_ref, tiles_held_ref, sems) = refs[:CHUNKS], refs[CHUNKS:]
    core = lax.axis_index("act")
    blocks, acts_here = tiles_held_ref.shape[1], tiles_held_ref.shape[0]
    own_tiles = tiles_ref.at[:, pl.ds(pl.multiple_of(core * blocks, blocks), blocks)]
    copies = [
        pltpu.make_async_copy(half_of(targets_ref, 1 - core), held_ref, sems.at[0]),
        pltpu.make_async_copy(own_tiles, tiles_held_ref, sems.at[1]),
    ]
    for copy in copies:
        copy.start()
    fill_slots(columns_ref, slots_ref)
    turn_tiles(taken_ref, core * blocks, right_ref, acts_here)
    for copy in copies:
        copy.wait()
    turn_targets(held_ref, out_refs)
    turn_tiles(tiles_held_ref, 0, right_ref, 0)


def fill_slots(columns_ref, out_ref):
    actions, _, row_blocks = columns_ref.shape
    blocks, half = row_blocks // 2, actions // 2
    total = row_blocks * lax.axis_size("states")
    core = lax.axis_index("act")
    start = lax.axis_index("states") * row_blocks + core * blocks - blocks
    for n in range(actions):
        action = (core if n < half else 1 - core) * half + n % half
        for b in range(blocks):
            for t in range(2):
                slot = columns_ref[action, t, core * blocks + b] - start
                slot = jnp.where(slot < 0, slot + total, slot)
                out_ref[(n * blocks + b) * 2 + t] = jnp.where(slot >= total, slot - total, slot)


def sweep_kernel(slot_ref, right_ref, own_ref, ici_ref, sib_ref, target_ref, out_ref, parts_ref):
    blocks, width, lanes = own_ref.shape
    core = lax.axis_index("act")
    for place, ref in ((1, own_ref), (2 - 2 * core, sib_ref), (2 * core, ici_ref)):
        for b in range(blocks):
            high, low = split(ref[b])
            parts_ref[place * blocks + b, :width] = high
            parts_ref[place * blocks + b, width:] = low
    for b in range(blocks):
        largest = None
        for a in range(right_ref.shape[1]):
            at = (a * blocks + b) * 2
            left = jnp.concatenate([parts_ref[slot_ref[at]], parts_ref[slot_ref[at + 1]]], axis=1)
            both = jnp.dot(left, right_ref[b, a], preferred_element_type=jnp.float32)
            q = (both[:width, :lanes] + both[:width, lanes:]) + (both[width:, :lanes] + both[width:, lanes:])
            largest = q if largest is None else jnp.maximum(largest, q)
        out_ref[b] = jnp.where(target_ref[b] == 1.0, 1.0, largest)


def finish_kernel(*refs):
    own_refs, sib_refs, (out_ref, held_ref, sems) = refs[:CHUNKS], refs[CHUNKS : 2 * CHUNKS], refs[2 * CHUNKS :]
    blocks, width, lanes = own_refs[0].shape
    core = lax.axis_index("act")
    one = unit(lanes, 3)
    copies = []
    for n, (part, group) in enumerate(((core, own_refs), (1 - core, sib_refs))):
        for b in range(blocks):
            panel = jnp.concatenate([ref[b] for ref in group], axis=0)
            high = panel.astype(jnp.bfloat16)
            middle, low = split(panel - high.astype(jnp.float32))
            held_ref[n, b * lanes : (b + 1) * lanes] = times_turned(one, jnp.concatenate([high, middle, low], axis=1))
        copies.append(pltpu.make_async_copy(held_ref.at[n], half_of(out_ref, part), sems.at[n]))
        copies[-1].start()
    for copy in copies:
        copy.wait()


def per_device(transitions, columns, targets):
    acts_here, row_blocks, _, lanes, _ = transitions.shape
    sets = targets.shape[1]
    width = sets // CHUNKS
    blocks = row_blocks // 2
    devices = 2 * lax.axis_size("states")

    to_sib = [(i, i ^ 1) for i in range(devices)]
    to_ici = [(i, (i + 1) % devices if i % 2 else (i - 1) % devices) for i in range(devices)]
    chunk = jax.ShapeDtypeStruct((blocks, width, lanes), jnp.float32)

    taken = lax.ppermute(transitions, AXES, to_sib)

    panel = pltpu.VMEM((blocks * lanes, sets), jnp.int32)
    targets = pltpu.with_memory_space_constraint(targets, HBM)
    zero = pl.pallas_call(
        own_kernel,
        out_shape=[chunk] * CHUNKS,
        in_specs=[ANYWHERE],
        out_specs=[WHOLE] * CHUNKS,
        scratch_shapes=[panel, pltpu.SemaphoreType.DMA],
        name="own_targets",
        compiler_params=pltpu.CompilerParams(vmem_limit_bytes=4 << 20),
    )(targets)
    ici = [lax.ppermute(v, AXES, to_ici) for v in zero]

    slots, right, *sib = pl.pallas_call(
        rest_kernel,
        out_shape=[
            SMEM((2 * acts_here * blocks * 2,), jnp.int32),
            jax.ShapeDtypeStruct((blocks, 2 * acts_here, 2 * lanes, 2 * lanes), jnp.bfloat16),
        ]
        + [chunk] * CHUNKS,
        in_specs=[SCALARS, ANYWHERE, ANYWHERE, WHOLE],
        out_specs=[SCALARS] + [WHOLE] * (1 + CHUNKS),
        scratch_shapes=[panel, pltpu.VMEM((acts_here, blocks, 2, lanes, lanes), jnp.float32), pltpu.SemaphoreType.DMA((2,))],
        name="rest",
        compiler_params=pltpu.CompilerParams(vmem_limit_bytes=16 << 20),
    )(columns.transpose(0, 2, 1), targets, pltpu.with_memory_space_constraint(transitions, HBM), taken)
    slots = pltpu.with_memory_space_constraint(slots, SMEM)

    def sweep(own, sib, ici, zero):
        return pl.pallas_call(
            sweep_kernel,
            out_shape=chunk,
            in_specs=[SCALARS] + [WHOLE] * 5,
            out_specs=WHOLE,
            scratch_shapes=[pltpu.VMEM((3 * blocks, 2 * width, lanes), jnp.bfloat16)],
            name="sweep",
            compiler_params=pltpu.CompilerParams(vmem_limit_bytes=16 << 20),
            cost_estimate=pl.CostEstimate(
                flops=2 * 2 * acts_here * blocks * (2 * width) * (2 * lanes) ** 2,
                bytes_accessed=4 * 5 * blocks * width * lanes + 8 * acts_here * blocks * (2 * lanes) ** 2,
                transcendentals=0,
            ),
        )(slots, right, own, ici, sib, zero)

    zero, own = list(zero), list(zero)
    for step in range(SWEEPS):
        for c in range(CHUNKS):
            own[c] = sweep(own[c], sib[c], ici[c], zero[c])
            if step < SWEEPS - 1:
                ici[c] = lax.ppermute(own[c], AXES, to_ici)
            sib[c] = lax.ppermute(own[c], AXES, to_sib)

    return pl.pallas_call(
        finish_kernel,
        out_shape=jax.ShapeDtypeStruct((2 * blocks * lanes, sets), jnp.float32),
        in_specs=[WHOLE] * (2 * CHUNKS),
        out_specs=ANYWHERE,
        scratch_shapes=[pltpu.VMEM((2, blocks * lanes, sets), jnp.float32), pltpu.SemaphoreType.DMA((2,))],
        name="finish",
        compiler_params=pltpu.CompilerParams(vmem_limit_bytes=8 << 20),
    )(*own, *sib)


def solution(mesh):
    return jax.shard_map(
        per_device,
        mesh=mesh,
        in_specs=(P("act", "states", None, None, None), P(None, "states", None), P("states", None)),
        out_specs=P("states", None),
        check_vma=False,
    )
```

```python
import jax
import jax.numpy as jnp
from jax import lax
from jax.experimental import pallas as pl
from jax.experimental.pallas import tpu as pltpu
from jax.sharding import PartitionSpec as P

SWEEPS = 12
CHUNKS = 2
UNIT = 16
AXES = ("states", "act")
VMEM = pltpu.VMEM
SMEM = pltpu.SMEM
HBM = pltpu.HBM
WHOLE = pl.BlockSpec(memory_space=VMEM)
SCALARS = pl.BlockSpec(memory_space=SMEM)
ANYWHERE = pl.BlockSpec(memory_space=pl.ANY)


def split(x):
    high = x.astype(jnp.bfloat16)
    return high, (x - high.astype(jnp.float32)).astype(jnp.bfloat16)


def unit(rows, repeats=1):
    row = lax.broadcasted_iota(jnp.int32, (rows, rows), 0)
    col = lax.broadcasted_iota(jnp.int32, (rows, rows), 1)
    one = jnp.where(row == col, 1.0, 0.0).astype(jnp.bfloat16)
    return jnp.concatenate([one] * repeats, axis=1)


def times_turned(left, right):
    return lax.dot_general(left, right, (((1,), (1,)), ((), ())), preferred_element_type=jnp.float32)


def turn_targets(held_ref, out_refs):
    blocks, _, lanes = out_refs[0].shape
    one = unit(held_ref.shape[1])
    for b in range(blocks):
        hit = held_ref[b * lanes : (b + 1) * lanes, :].astype(jnp.float32).astype(jnp.bfloat16)
        turned = times_turned(one, hit)
        at = 0
        for out_ref in out_refs:
            out_ref[b] = turned[at : at + out_ref.shape[1]]
            at += out_ref.shape[1]


def half_of(ref, part):
    rows = ref.shape[0] // 2
    return ref.at[pl.ds(pl.multiple_of(part * rows, rows), rows)]


def own_kernel(targets_ref, columns_ref, columns_out_ref, *refs):
    out_refs, (held_ref, sems) = refs[:CHUNKS], refs[CHUNKS:]
    copies = [
        pltpu.make_async_copy(half_of(targets_ref, lax.axis_index("act")), held_ref, sems.at[0]),
        pltpu.make_async_copy(columns_ref, columns_out_ref, sems.at[1]),
    ]
    for copy in copies:
        copy.start()
    for copy in copies:
        copy.wait()
    turn_targets(held_ref, out_refs)


def turn_tiles(tiles_ref, first, out_ref, start):
    blocks, _, side, _ = out_ref.shape
    lanes = side // 2
    one = unit(lanes)
    for b in range(blocks):
        for a in range(tiles_ref.shape[0]):
            for t in range(2):
                both = jnp.concatenate(split(tiles_ref[a, first + b, t]), axis=0)
                out_ref[b, start + a, t * lanes : (t + 1) * lanes] = times_turned(one, both).astype(jnp.bfloat16)


def rest_kernel(columns_ref, targets_ref, tiles_ref, taken_ref, slots_ref, right_ref, *refs):
    out_refs, (held_ref, tiles_held_ref, sems) = refs[:CHUNKS], refs[CHUNKS:]
    core = lax.axis_index("act")
    blocks, acts_here = tiles_held_ref.shape[1], tiles_held_ref.shape[0]
    own_tiles = tiles_ref.at[:, pl.ds(pl.multiple_of(core * blocks, blocks), blocks)]
    copies = [
        pltpu.make_async_copy(half_of(targets_ref, 1 - core), held_ref, sems.at[0]),
        pltpu.make_async_copy(own_tiles, tiles_held_ref, sems.at[1]),
    ]
    for copy in copies:
        copy.start()
    fill_slots(columns_ref, slots_ref)
    turn_tiles(taken_ref, core * blocks, right_ref, acts_here)
    for copy in copies:
        copy.wait()
    turn_targets(held_ref, out_refs)
    turn_tiles(tiles_held_ref, 0, right_ref, 0)


def fill_slots(columns_ref, out_ref):
    actions, _, row_blocks = columns_ref.shape
    blocks, half = row_blocks // 2, actions // 2
    total = row_blocks * lax.axis_size("states")
    core = lax.axis_index("act")
    start = lax.axis_index("states") * row_blocks + core * blocks - blocks
    for n in range(actions):
        action = (core if n < half else 1 - core) * half + n % half
        for b in range(blocks):
            for t in range(2):
                slot = columns_ref[action, t, core * blocks + b] - start
                slot = jnp.where(slot < 0, slot + total, slot)
                out_ref[(n * blocks + b) * 2 + t] = jnp.where(slot >= total, slot - total, slot)


def sweep_kernel(slot_ref, right_ref, own_ref, ici_ref, sib_ref, target_ref, out_ref, parts_ref):
    blocks, width, lanes = own_ref.shape
    core = lax.axis_index("act")
    for place, ref in ((1, own_ref), (2 - 2 * core, sib_ref), (2 * core, ici_ref)):
        for b in range(blocks):
            high, low = split(ref[b])
            parts_ref[place * blocks + b, :width] = high
            parts_ref[place * blocks + b, width:] = low
    for b in range(blocks):
        largest = None
        for a in range(right_ref.shape[1]):
            at = (a * blocks + b) * 2
            left = jnp.concatenate([parts_ref[slot_ref[at]], parts_ref[slot_ref[at + 1]]], axis=1)
            both = jnp.dot(left, right_ref[b, a], preferred_element_type=jnp.float32)
            q = (both[:width, :lanes] + both[:width, lanes:]) + (both[width:, :lanes] + both[width:, lanes:])
            largest = q if largest is None else jnp.maximum(largest, q)
        out_ref[b] = jnp.where(target_ref[b] == 1.0, 1.0, largest)


def finish_kernel(*refs):
    own_refs, sib_refs, (out_ref, held_ref, sems) = refs[:CHUNKS], refs[CHUNKS : 2 * CHUNKS], refs[2 * CHUNKS :]
    blocks, _, lanes = own_refs[0].shape
    core = lax.axis_index("act")
    one = unit(lanes, 3)
    copies = []
    for n, (part, group) in enumerate(((core, own_refs), (1 - core, sib_refs))):
        for b in range(blocks):
            panel = jnp.concatenate([ref[b] for ref in group], axis=0)
            high = panel.astype(jnp.bfloat16)
            middle, low = split(panel - high.astype(jnp.float32))
            held_ref[n, b * lanes : (b + 1) * lanes] = times_turned(one, jnp.concatenate([high, middle, low], axis=1))
        copies.append(pltpu.make_async_copy(held_ref.at[n], half_of(out_ref, part), sems.at[n]))
        copies[-1].start()
    for copy in copies:
        copy.wait()


def per_device(transitions, columns, targets):
    acts_here, row_blocks, _, lanes, _ = transitions.shape
    sets = targets.shape[1]
    widths = [min(UNIT * -(-sets // (UNIT * CHUNKS)), sets - c * UNIT * -(-sets // (UNIT * CHUNKS))) for c in range(CHUNKS)]
    blocks = row_blocks // 2
    devices = 2 * lax.axis_size("states")

    to_sib = [(i, i ^ 1) for i in range(devices)]
    to_ici = [(i, (i + 1) % devices if i % 2 else (i - 1) % devices) for i in range(devices)]
    chunks = [jax.ShapeDtypeStruct((blocks, width, lanes), jnp.float32) for width in widths]

    taken = lax.ppermute(transitions, AXES, to_sib)

    panel = pltpu.VMEM((blocks * lanes, sets), jnp.int32)
    targets = pltpu.with_memory_space_constraint(targets, HBM)
    columns = columns.transpose(0, 2, 1)
    columns, *zero = pl.pallas_call(
        own_kernel,
        out_shape=[SMEM(columns.shape, jnp.int32)] + chunks,
        in_specs=[ANYWHERE] * 2,
        out_specs=[SCALARS] + [WHOLE] * CHUNKS,
        scratch_shapes=[panel, pltpu.SemaphoreType.DMA((2,))],
        name="own_targets",
        compiler_params=pltpu.CompilerParams(vmem_limit_bytes=4 << 20),
    )(targets, pltpu.with_memory_space_constraint(columns, HBM))
    ici = [lax.ppermute(v, AXES, to_ici) for v in zero]

    slots, right, *sib = pl.pallas_call(
        rest_kernel,
        out_shape=[
            SMEM((2 * acts_here * blocks * 2,), jnp.int32),
            jax.ShapeDtypeStruct((blocks, 2 * acts_here, 2 * lanes, 2 * lanes), jnp.bfloat16),
        ]
        + chunks,
        in_specs=[SCALARS, ANYWHERE, ANYWHERE, WHOLE],
        out_specs=[SCALARS] + [WHOLE] * (1 + CHUNKS),
        scratch_shapes=[panel, pltpu.VMEM((acts_here, blocks, 2, lanes, lanes), jnp.float32), pltpu.SemaphoreType.DMA((2,))],
        name="rest",
        compiler_params=pltpu.CompilerParams(vmem_limit_bytes=16 << 20),
    )(pltpu.with_memory_space_constraint(columns, SMEM), targets, pltpu.with_memory_space_constraint(transitions, HBM), taken)
    slots = pltpu.with_memory_space_constraint(slots, SMEM)

    def sweep(own, sib, ici, zero):
        width = own.shape[1]
        return pl.pallas_call(
            sweep_kernel,
            out_shape=jax.ShapeDtypeStruct(own.shape, jnp.float32),
            in_specs=[SCALARS] + [WHOLE] * 5,
            out_specs=WHOLE,
            scratch_shapes=[pltpu.VMEM((3 * blocks, 2 * width, lanes), jnp.bfloat16)],
            name="sweep",
            compiler_params=pltpu.CompilerParams(vmem_limit_bytes=16 << 20),
            cost_estimate=pl.CostEstimate(
                flops=2 * 2 * acts_here * blocks * (2 * width) * (2 * lanes) ** 2,
                bytes_accessed=4 * 5 * blocks * width * lanes + 8 * acts_here * blocks * (2 * lanes) ** 2,
                transcendentals=0,
            ),
        )(slots, right, own, ici, sib, zero)

    zero, own = list(zero), list(zero)
    for step in range(SWEEPS):
        for c in range(CHUNKS):
            own[c] = sweep(own[c], sib[c], ici[c], zero[c])
            if step < SWEEPS - 1:
                ici[c] = lax.ppermute(own[c], AXES, to_ici)
            sib[c] = lax.ppermute(own[c], AXES, to_sib)
            if step < SWEEPS - 1 or c < CHUNKS - 1:
                n = (c + 1) % CHUNKS
                ici[n], sib[c] = lax.optimization_barrier((ici[n], sib[c]))

    return pl.pallas_call(
        finish_kernel,
        out_shape=jax.ShapeDtypeStruct((2 * blocks * lanes, sets), jnp.float32),
        in_specs=[WHOLE] * (2 * CHUNKS),
        out_specs=ANYWHERE,
        scratch_shapes=[pltpu.VMEM((2, blocks * lanes, sets), jnp.float32), pltpu.SemaphoreType.DMA((2,))],
        name="finish",
        compiler_params=pltpu.CompilerParams(vmem_limit_bytes=8 << 20),
    )(*own, *sib)


def solution(mesh):
    return jax.shard_map(
        per_device,
        mesh=mesh,
        in_specs=(P("act", "states", None, None, None), P(None, "states", None), P("states", None)),
        out_specs=P("states", None),
        check_vma=False,
    )
```

```python
import functools

import jax
import jax.numpy as jnp
from jax import lax
from jax.experimental import pallas as pl
from jax.experimental.pallas import tpu as pltpu
from jax.sharding import PartitionSpec as P

SWEEPS = 12
CHUNKS = 2
UNIT = 16
AXES = ("states", "act")
VMEM = pltpu.VMEM
SMEM = pltpu.SMEM
HBM = pltpu.HBM
WHOLE = pl.BlockSpec(memory_space=VMEM)
SCALARS = pl.BlockSpec(memory_space=SMEM)
ANYWHERE = pl.BlockSpec(memory_space=pl.ANY)


def split(x):
    high = x.astype(jnp.bfloat16)
    return high, (x - high.astype(jnp.float32)).astype(jnp.bfloat16)


def unit(rows, repeats=1):
    row = lax.broadcasted_iota(jnp.int32, (rows, rows), 0)
    col = lax.broadcasted_iota(jnp.int32, (rows, rows), 1)
    one = jnp.where(row == col, 1.0, 0.0).astype(jnp.bfloat16)
    return jnp.concatenate([one] * repeats, axis=1)


def times_turned(left, right):
    return lax.dot_general(left, right, (((1,), (1,)), ((), ())), preferred_element_type=jnp.float32)


def turn_targets(held_ref, out_refs):
    blocks, _, lanes = out_refs[0].shape
    one = unit(held_ref.shape[1])
    for b in range(blocks):
        hit = held_ref[b * lanes : (b + 1) * lanes, :].astype(jnp.float32).astype(jnp.bfloat16)
        turned = times_turned(one, hit)
        at = 0
        for out_ref in out_refs:
            out_ref[b] = turned[at : at + out_ref.shape[1]]
            at += out_ref.shape[1]


def half_of(ref, part):
    rows = ref.shape[0] // 2
    return ref.at[pl.ds(pl.multiple_of(part * rows, rows), rows)]


def own_kernel(targets_ref, columns_ref, columns_out_ref, *refs):
    out_refs, (held_ref, sems) = refs[:CHUNKS], refs[CHUNKS:]
    copies = [
        pltpu.make_async_copy(half_of(targets_ref, lax.axis_index("act")), held_ref, sems.at[0]),
        pltpu.make_async_copy(columns_ref, columns_out_ref, sems.at[1]),
    ]
    for copy in copies:
        copy.start()
    for copy in copies:
        copy.wait()
    turn_targets(held_ref, out_refs)


def turn_tiles(tiles_ref, first, out_ref, start):
    blocks, _, side, _ = out_ref.shape
    lanes = side // 2
    one = unit(lanes)
    for b in range(blocks):
        for a in range(tiles_ref.shape[0]):
            for t in range(2):
                both = jnp.concatenate(split(tiles_ref[a, first + b, t]), axis=0)
                out_ref[b, start + a, t * lanes : (t + 1) * lanes] = times_turned(one, both).astype(jnp.bfloat16)


def rest_kernel(columns_ref, targets_ref, tiles_ref, taken_ref, slots_ref, right_ref, *refs):
    out_refs, (held_ref, tiles_held_ref, sems) = refs[:CHUNKS], refs[CHUNKS:]
    core = lax.axis_index("act")
    blocks, acts_here = tiles_held_ref.shape[1], tiles_held_ref.shape[0]
    own_tiles = tiles_ref.at[:, pl.ds(pl.multiple_of(core * blocks, blocks), blocks)]
    copies = [
        pltpu.make_async_copy(half_of(targets_ref, 1 - core), held_ref, sems.at[0]),
        pltpu.make_async_copy(own_tiles, tiles_held_ref, sems.at[1]),
    ]
    for copy in copies:
        copy.start()
    fill_slots(columns_ref, slots_ref)
    turn_tiles(taken_ref, core * blocks, right_ref, acts_here)
    for copy in copies:
        copy.wait()
    turn_targets(held_ref, out_refs)
    turn_tiles(tiles_held_ref, 0, right_ref, 0)


def fill_slots(columns_ref, out_ref):
    actions, _, row_blocks = columns_ref.shape
    blocks, half = row_blocks // 2, actions // 2
    total = row_blocks * lax.axis_size("states")
    core = lax.axis_index("act")
    start = lax.axis_index("states") * row_blocks + core * blocks - blocks
    for n in range(actions):
        action = (core if n < half else 1 - core) * half + n % half
        for b in range(blocks):
            for t in range(2):
                slot = columns_ref[action, t, core * blocks + b] - start
                slot = jnp.where(slot < 0, slot + total, slot)
                out_ref[(n * blocks + b) * 2 + t] = jnp.where(slot >= total, slot - total, slot)


def sweep_kernel(slot_ref, right_ref, own_ref, ici_ref, sib_ref, target_ref, out_ref, parts_ref):
    blocks, width, lanes = own_ref.shape
    core = lax.axis_index("act")
    for place, ref in ((1, own_ref), (2 - 2 * core, sib_ref), (2 * core, ici_ref)):
        for b in range(blocks):
            high, low = split(ref[b])
            parts_ref[place * blocks + b, :width] = high
            parts_ref[place * blocks + b, width:] = low
    for b in range(blocks):
        largest = None
        for a in range(right_ref.shape[1]):
            at = (a * blocks + b) * 2
            left = jnp.concatenate([parts_ref[slot_ref[at]], parts_ref[slot_ref[at + 1]]], axis=1)
            both = jnp.dot(left, right_ref[b, a], preferred_element_type=jnp.float32)
            q = (both[:width, :lanes] + both[:width, lanes:]) + (both[width:, :lanes] + both[width:, lanes:])
            largest = q if largest is None else jnp.maximum(largest, q)
        out_ref[b] = jnp.where(target_ref[b] == 1.0, 1.0, largest)


def finish_kernel(other, *refs):
    chunk_refs, (out_ref, held_ref, sem) = refs[:CHUNKS], refs[-3:]
    blocks, _, lanes = chunk_refs[0].shape
    core = lax.axis_index("act")
    one = unit(lanes, 3)
    for b in range(blocks):
        panel = jnp.concatenate([ref[b] for ref in chunk_refs], axis=0)
        high = panel.astype(jnp.bfloat16)
        middle, low = split(panel - high.astype(jnp.float32))
        held_ref[b * lanes : (b + 1) * lanes] = times_turned(one, jnp.concatenate([high, middle, low], axis=1))
    copy = pltpu.make_async_copy(held_ref, half_of(out_ref, 1 - core if other else core), sem)
    copy.start()
    copy.wait()


def per_device(transitions, columns, targets):
    acts_here, row_blocks, _, lanes, _ = transitions.shape
    sets = targets.shape[1]
    widths = [min(UNIT * -(-sets // (UNIT * CHUNKS)), sets - c * UNIT * -(-sets // (UNIT * CHUNKS))) for c in range(CHUNKS)]
    blocks = row_blocks // 2
    devices = 2 * lax.axis_size("states")

    to_sib = [(i, i ^ 1) for i in range(devices)]
    to_ici = [(i, (i + 1) % devices if i % 2 else (i - 1) % devices) for i in range(devices)]
    chunks = [jax.ShapeDtypeStruct((blocks, width, lanes), jnp.float32) for width in widths]

    taken = lax.ppermute(transitions, AXES, to_sib)

    panel = pltpu.VMEM((blocks * lanes, sets), jnp.int32)
    targets = pltpu.with_memory_space_constraint(targets, HBM)
    columns = columns.transpose(0, 2, 1)
    columns, *zero = pl.pallas_call(
        own_kernel,
        out_shape=[SMEM(columns.shape, jnp.int32)] + chunks,
        in_specs=[ANYWHERE] * 2,
        out_specs=[SCALARS] + [WHOLE] * CHUNKS,
        scratch_shapes=[panel, pltpu.SemaphoreType.DMA((2,))],
        name="own_targets",
        compiler_params=pltpu.CompilerParams(vmem_limit_bytes=4 << 20),
    )(targets, pltpu.with_memory_space_constraint(columns, HBM))
    ici = [lax.ppermute(v, AXES, to_ici) for v in zero]

    slots, right, *sib = pl.pallas_call(
        rest_kernel,
        out_shape=[
            SMEM((2 * acts_here * blocks * 2,), jnp.int32),
            jax.ShapeDtypeStruct((blocks, 2 * acts_here, 2 * lanes, 2 * lanes), jnp.bfloat16),
        ]
        + chunks,
        in_specs=[SCALARS, ANYWHERE, ANYWHERE, WHOLE],
        out_specs=[SCALARS] + [WHOLE] * (1 + CHUNKS),
        scratch_shapes=[panel, pltpu.VMEM((acts_here, blocks, 2, lanes, lanes), jnp.float32), pltpu.SemaphoreType.DMA((2,))],
        name="rest",
        compiler_params=pltpu.CompilerParams(vmem_limit_bytes=16 << 20),
    )(pltpu.with_memory_space_constraint(columns, SMEM), targets, pltpu.with_memory_space_constraint(transitions, HBM), taken)
    slots = pltpu.with_memory_space_constraint(slots, SMEM)

    def sweep(own, sib, ici, zero):
        width = own.shape[1]
        return pl.pallas_call(
            sweep_kernel,
            out_shape=jax.ShapeDtypeStruct(own.shape, jnp.float32),
            in_specs=[SCALARS] + [WHOLE] * 5,
            out_specs=WHOLE,
            scratch_shapes=[pltpu.VMEM((3 * blocks, 2 * width, lanes), jnp.bfloat16)],
            name="sweep",
            compiler_params=pltpu.CompilerParams(vmem_limit_bytes=16 << 20),
            cost_estimate=pl.CostEstimate(
                flops=2 * 2 * acts_here * blocks * (2 * width) * (2 * lanes) ** 2,
                bytes_accessed=4 * 5 * blocks * width * lanes + 8 * acts_here * blocks * (2 * lanes) ** 2,
                transcendentals=0,
            ),
        )(slots, right, own, ici, sib, zero)

    zero, own = list(zero), list(zero)
    for step in range(SWEEPS):
        for c in range(CHUNKS):
            own[c] = sweep(own[c], sib[c], ici[c], zero[c])
            if step < SWEEPS - 1:
                ici[c] = lax.ppermute(own[c], AXES, to_ici)
            sib[c] = lax.ppermute(own[c], AXES, to_sib)
            if step < SWEEPS - 1 or c < CHUNKS - 1:
                n = (c + 1) % CHUNKS
                ici[n], sib[c] = lax.optimization_barrier((ici[n], sib[c]))

    def finish(other, chunks, *half):
        return pl.pallas_call(
            functools.partial(finish_kernel, other),
            out_shape=jax.ShapeDtypeStruct((2 * blocks * lanes, sets), jnp.float32),
            in_specs=[WHOLE] * CHUNKS + [ANYWHERE] * len(half),
            out_specs=ANYWHERE,
            scratch_shapes=[pltpu.VMEM((blocks * lanes, sets), jnp.float32), pltpu.SemaphoreType.DMA],
            input_output_aliases={CHUNKS: 0} if half else {},
            name="finish",
            compiler_params=pltpu.CompilerParams(vmem_limit_bytes=8 << 20),
        )(*chunks, *half)

    return finish(True, sib, finish(False, own))


def solution(mesh):
    return jax.shard_map(
        per_device,
        mesh=mesh,
        in_specs=(P("act", "states", None, None, None), P(None, "states", None), P("states", None)),
        out_specs=P("states", None),
        check_vma=False,
    )
```

```python
import functools

import jax
import jax.numpy as jnp
from jax import lax
from jax.experimental import pallas as pl
from jax.experimental.pallas import tpu as pltpu
from jax.sharding import PartitionSpec as P

SWEEPS = 12
CHUNKS = 2
UNIT = 16
AXES = ("states", "act")
VMEM = pltpu.VMEM
SMEM = pltpu.SMEM
HBM = pltpu.HBM
WHOLE = pl.BlockSpec(memory_space=VMEM)
SCALARS = pl.BlockSpec(memory_space=SMEM)
ANYWHERE = pl.BlockSpec(memory_space=pl.ANY)


def split(x):
    high = x.astype(jnp.bfloat16)
    return high, (x - high.astype(jnp.float32)).astype(jnp.bfloat16)


def unit(rows, repeats=1):
    row = lax.broadcasted_iota(jnp.int32, (rows, rows), 0)
    col = lax.broadcasted_iota(jnp.int32, (rows, rows), 1)
    one = jnp.where(row == col, 1.0, 0.0).astype(jnp.bfloat16)
    return jnp.concatenate([one] * repeats, axis=1)


def times_turned(left, right):
    return lax.dot_general(left, right, (((1,), (1,)), ((), ())), preferred_element_type=jnp.float32)


def turn_targets(held_ref, out_refs):
    blocks, _, lanes = out_refs[0].shape
    one = unit(held_ref.shape[1])
    for b in range(blocks):
        hit = held_ref[b * lanes : (b + 1) * lanes, :].astype(jnp.float32).astype(jnp.bfloat16)
        turned = times_turned(one, hit)
        at = 0
        for out_ref in out_refs:
            out_ref[b] = turned[at : at + out_ref.shape[1]]
            at += out_ref.shape[1]


def half_of(ref, part):
    rows = ref.shape[0] // 2
    return ref.at[pl.ds(pl.multiple_of(part * rows, rows), rows)]


def own_kernel(targets_ref, columns_ref, columns_out_ref, *refs):
    out_refs, (held_ref, sems) = refs[:CHUNKS], refs[CHUNKS:]
    copies = [
        pltpu.make_async_copy(half_of(targets_ref, lax.axis_index("act")), held_ref, sems.at[0]),
        pltpu.make_async_copy(columns_ref, columns_out_ref, sems.at[1]),
    ]
    for copy in copies:
        copy.start()
    for copy in copies:
        copy.wait()
    turn_targets(held_ref, out_refs)


def turn_tiles(tiles_ref, first, out_ref, start):
    blocks, _, side, _ = out_ref.shape
    lanes = side // 2
    one = unit(lanes)
    for b in range(blocks):
        for a in range(tiles_ref.shape[0]):
            for t in range(2):
                both = jnp.concatenate(split(tiles_ref[a, first + b, t]), axis=0)
                out_ref[b, start + a, t * lanes : (t + 1) * lanes] = times_turned(one, both).astype(jnp.bfloat16)


def rest_kernel(columns_ref, targets_ref, tiles_ref, taken_ref, slots_ref, right_ref, *refs):
    out_refs, (held_ref, tiles_held_ref, sems) = refs[:CHUNKS], refs[CHUNKS:]
    core = lax.axis_index("act")
    blocks, acts_here = tiles_held_ref.shape[1], tiles_held_ref.shape[0]
    own_tiles = tiles_ref.at[:, pl.ds(pl.multiple_of(core * blocks, blocks), blocks)]
    copies = [
        pltpu.make_async_copy(half_of(targets_ref, 1 - core), held_ref, sems.at[0]),
        pltpu.make_async_copy(own_tiles, tiles_held_ref, sems.at[1]),
    ]
    for copy in copies:
        copy.start()
    fill_slots(columns_ref, slots_ref)
    turn_tiles(taken_ref, core * blocks, right_ref, acts_here)
    for copy in copies:
        copy.wait()
    turn_targets(held_ref, out_refs)
    turn_tiles(tiles_held_ref, 0, right_ref, 0)


def fill_slots(columns_ref, out_ref):
    actions, _, row_blocks = columns_ref.shape
    blocks, half = row_blocks // 2, actions // 2
    total = row_blocks * lax.axis_size("states")
    core = lax.axis_index("act")
    start = lax.axis_index("states") * row_blocks + core * blocks - blocks
    for n in range(actions):
        action = (core if n < half else 1 - core) * half + n % half
        for b in range(blocks):
            for t in range(2):
                slot = columns_ref[action, t, core * blocks + b] - start
                slot = jnp.where(slot < 0, slot + total, slot)
                out_ref[(n * blocks + b) * 2 + t] = jnp.where(slot >= total, slot - total, slot)


def sweep_kernel(slot_ref, right_ref, own_ref, ici_ref, sib_ref, target_ref, out_ref, parts_ref):
    blocks, width, lanes = own_ref.shape
    core = lax.axis_index("act")
    for place, ref in ((1, own_ref), (2 - 2 * core, sib_ref), (2 * core, ici_ref)):
        for b in range(blocks):
            high, low = split(ref[b])
            parts_ref[place * blocks + b, :width] = high
            parts_ref[place * blocks + b, width:] = low
    for b in range(blocks):
        largest = None
        for a in range(right_ref.shape[1]):
            at = (a * blocks + b) * 2
            left = jnp.concatenate([parts_ref[slot_ref[at]], parts_ref[slot_ref[at + 1]]], axis=1)
            both = jnp.dot(left, right_ref[b, a], preferred_element_type=jnp.float32)
            q = (both[:width, :lanes] + both[:width, lanes:]) + (both[width:, :lanes] + both[width:, lanes:])
            largest = q if largest is None else jnp.maximum(largest, q)
        out_ref[b] = jnp.where(target_ref[b] == 1.0, 1.0, largest)


def finish_kernel(other, *refs):
    chunk_refs, (out_ref, held_ref, sems) = refs[:CHUNKS], refs[-3:]
    blocks, _, lanes = chunk_refs[0].shape
    core = lax.axis_index("act")
    one = unit(lanes, 3)
    half_ref = half_of(out_ref, 1 - core if other else core)
    rows = blocks * lanes // 2
    copies = []
    for b in range(blocks):
        panel = jnp.concatenate([ref[b] for ref in chunk_refs], axis=0)
        high = panel.astype(jnp.bfloat16)
        middle, low = split(panel - high.astype(jnp.float32))
        held_ref[b * lanes : (b + 1) * lanes] = times_turned(one, jnp.concatenate([high, middle, low], axis=1))
        if (b + 1) % (blocks // 2) == 0:
            n = len(copies)
            part = pl.ds(n * rows, rows)
            copies.append(pltpu.make_async_copy(held_ref.at[part], half_ref.at[part], sems.at[n]))
            copies[-1].start()
    for copy in copies:
        copy.wait()


def per_device(transitions, columns, targets):
    acts_here, row_blocks, _, lanes, _ = transitions.shape
    sets = targets.shape[1]
    widths = [min(UNIT * -(-sets // (UNIT * CHUNKS)), sets - c * UNIT * -(-sets // (UNIT * CHUNKS))) for c in range(CHUNKS)]
    blocks = row_blocks // 2
    devices = 2 * lax.axis_size("states")

    to_sib = [(i, i ^ 1) for i in range(devices)]
    to_ici = [(i, (i + 1) % devices if i % 2 else (i - 1) % devices) for i in range(devices)]
    chunks = [jax.ShapeDtypeStruct((blocks, width, lanes), jnp.float32) for width in widths]

    taken = lax.ppermute(transitions, AXES, to_sib)

    panel = pltpu.VMEM((blocks * lanes, sets), jnp.int32)
    targets = pltpu.with_memory_space_constraint(targets, HBM)
    columns = columns.transpose(0, 2, 1)
    columns, *zero = pl.pallas_call(
        own_kernel,
        out_shape=[SMEM(columns.shape, jnp.int32)] + chunks,
        in_specs=[ANYWHERE] * 2,
        out_specs=[SCALARS] + [WHOLE] * CHUNKS,
        scratch_shapes=[panel, pltpu.SemaphoreType.DMA((2,))],
        name="own_targets",
        compiler_params=pltpu.CompilerParams(vmem_limit_bytes=4 << 20),
    )(targets, pltpu.with_memory_space_constraint(columns, HBM))
    ici = [lax.ppermute(v, AXES, to_ici) for v in zero]

    slots, right, *sib = pl.pallas_call(
        rest_kernel,
        out_shape=[
            SMEM((2 * acts_here * blocks * 2,), jnp.int32),
            jax.ShapeDtypeStruct((blocks, 2 * acts_here, 2 * lanes, 2 * lanes), jnp.bfloat16),
        ]
        + chunks,
        in_specs=[SCALARS, ANYWHERE, ANYWHERE, WHOLE],
        out_specs=[SCALARS] + [WHOLE] * (1 + CHUNKS),
        scratch_shapes=[panel, pltpu.VMEM((acts_here, blocks, 2, lanes, lanes), jnp.float32), pltpu.SemaphoreType.DMA((2,))],
        name="rest",
        compiler_params=pltpu.CompilerParams(vmem_limit_bytes=16 << 20),
    )(pltpu.with_memory_space_constraint(columns, SMEM), targets, pltpu.with_memory_space_constraint(transitions, HBM), taken)
    slots = pltpu.with_memory_space_constraint(slots, SMEM)

    def sweep(own, sib, ici, zero):
        width = own.shape[1]
        return pl.pallas_call(
            sweep_kernel,
            out_shape=jax.ShapeDtypeStruct(own.shape, jnp.float32),
            in_specs=[SCALARS] + [WHOLE] * 5,
            out_specs=WHOLE,
            scratch_shapes=[pltpu.VMEM((3 * blocks, 2 * width, lanes), jnp.bfloat16)],
            name="sweep",
            compiler_params=pltpu.CompilerParams(vmem_limit_bytes=16 << 20),
            cost_estimate=pl.CostEstimate(
                flops=2 * 2 * acts_here * blocks * (2 * width) * (2 * lanes) ** 2,
                bytes_accessed=4 * 5 * blocks * width * lanes + 8 * acts_here * blocks * (2 * lanes) ** 2,
                transcendentals=0,
            ),
        )(slots, right, own, ici, sib, zero)

    zero, own = list(zero), list(zero)
    for step in range(SWEEPS):
        for c in range(CHUNKS):
            own[c] = sweep(own[c], sib[c], ici[c], zero[c])
            if step < SWEEPS - 1:
                ici[c] = lax.ppermute(own[c], AXES, to_ici)
            sib[c] = lax.ppermute(own[c], AXES, to_sib)
            if step < SWEEPS - 1 or c < CHUNKS - 1:
                n = (c + 1) % CHUNKS
                ici[n], sib[c] = lax.optimization_barrier((ici[n], sib[c]))

    def finish(other, chunks, *half):
        return pl.pallas_call(
            functools.partial(finish_kernel, other),
            out_shape=jax.ShapeDtypeStruct((2 * blocks * lanes, sets), jnp.float32),
            in_specs=[WHOLE] * CHUNKS + [ANYWHERE] * len(half),
            out_specs=ANYWHERE,
            scratch_shapes=[pltpu.VMEM((blocks * lanes, sets), jnp.float32), pltpu.SemaphoreType.DMA((2,))],
            input_output_aliases={CHUNKS: 0} if half else {},
            name="finish",
            compiler_params=pltpu.CompilerParams(vmem_limit_bytes=8 << 20),
        )(*chunks, *half)

    return finish(True, sib, finish(False, own))


def solution(mesh):
    return jax.shard_map(
        per_device,
        mesh=mesh,
        in_specs=(P("act", "states", None, None, None), P(None, "states", None), P("states", None)),
        out_specs=P("states", None),
        check_vma=False,
    )
```
